256 devices in a mesh: ctx: 64 (over y, z, core), batch: 4 (over x).
Axes of the slice: x: 4, y: 4, z: 8, core: 2. Of those that a mesh axis runs over, the one named last changes fastest.
Arguments:
- queries: float32 [4, 8192, 2048], P('batch', 'ctx'), may hold values from -8 to 8
- keys: float32 [4, 8192, 2048], P('batch', 'ctx'), may hold values from -8 to 8
- values: float32 [4, 8192, 2048], P('batch', 'ctx'), may hold values from -6 to 6
- kernel: float32 [16, 33], replicated, may hold values from -1.2 to 1.2
- cotangent: float32 [4, 8192, 2048], P('batch', 'ctx'), may hold values from -12 to 12
Outputs:
- mixed: float32 [4, 8192, 2048], P('batch', 'ctx')
- query_grad: float32 [4, 8192, 2048], P('batch', 'ctx')
- key_grad: float32 [4, 8192, 2048], P('batch', 'ctx')
- value_grad: float32 [4, 8192, 2048], P('batch', 'ctx')
- kernel_grad: float32 [16, 33], replicated
The draws below stay inside these ranges and needn't reach their ends.
All inputs are finite; a program needn't handle non-finite values.
Results may differ from the reference program's by a relative error of at most 0.0004.
Values sent between devices are 32-bit elements; how exact they have to be, the bound alone decides.
A program may use at most 256 MiB of HBM per device.

```python
import math
import jax
import jax.numpy as jnp
from jax import lax

HEAD_TOTAL = 16
HEAD_FEATURES = 128
M = 128
KS = 33
ITERS = 3
D = 2048
SEQUENCE_LENGTH = 8192
BATCH = 4


def smooth_field(key, coarse_scale):
    coarse_key = jax.random.fold_in(key, 21)
    fine_key = jax.random.fold_in(key, 22)
    coarse = coarse_scale * jax.random.normal(coarse_key, (BATCH, M, D))
    fine_part = jax.random.normal(fine_key, (BATCH, SEQUENCE_LENGTH, D))
    result_field = jnp.repeat(coarse, SEQUENCE_LENGTH // M, axis=1) + fine_part
    return jnp.clip(result_field, -8.0, 8.0)


def draw_queries(key, part):
    own_key = jax.random.fold_in(key, 1)
    return smooth_field(own_key, 1.5)


def draw_keys(key, part):
    own_key = jax.random.fold_in(key, 2)
    return smooth_field(own_key, 1.5)


def draw_cotangent(key, part):
    key = jax.random.fold_in(key, 3)
    position = jnp.arange(SEQUENCE_LENGTH, dtype=jnp.float32) / (SEQUENCE_LENGTH - 1)
    base_draw = jnp.clip(jax.random.normal(key, (BATCH, SEQUENCE_LENGTH, D)), -4.0, 4.0)
    ramp_scale = 1.0 + 2.0 * position
    return base_draw * ramp_scale[None, :, None]


def levels(stream_key, shape, cuts, least, largest):
    loudness, own = 1.0, jax.random.fold_in(stream_key, 6)
    for axis_at, parts in cuts:
        draws = jnp.exp(jax.random.uniform(jax.random.fold_in(own, axis_at), (parts,), jnp.float32, least / len(cuts), largest / len(cuts)))
        loudness = loudness * jnp.repeat(draws, shape[axis_at] // parts).reshape([-1 if axis == axis_at else 1 for axis in range(len(shape))])
    return loudness


def noise(rng, shape, spread, most, split=(), held_as=jnp.bfloat16):
    values = spread * jax.random.normal(rng, shape, jnp.float32)
    if split:
        values = values * levels(rng, shape, split, -0.22, 0.18)
    return jnp.clip(values, -most, most).astype(held_as)


def setup_inputs(seed: int = 0) -> dict:
    streams_of = jax.random.split(jax.random.key(seed), 6)
    return {
        "queries": draw_queries(jax.random.fold_in(streams_of[5], 71), 0),
        "keys": draw_keys(jax.random.fold_in(streams_of[5], 71), 0),
        "values": noise(streams_of[2], (BATCH, SEQUENCE_LENGTH, D), 1.0, 6.0, ((0, 4), (1, 64)), jnp.float32),
        "kernel": noise(streams_of[3], (HEAD_TOTAL, KS), 0.2, 1.2, (), jnp.float32),
        "cotangent": draw_cotangent(jax.random.fold_in(streams_of[5], 71), 0),
    }


def contract_product(pattern, former, latter):
    return jnp.einsum(pattern, former, latter, precision=lax.Precision.HIGHEST)

def row_softmax(scores):
    highest = lax.optimization_barrier(jnp.max(scores, axis=-1, keepdims=True))
    exponent = jnp.exp(scores - highest)
    return exponent / lax.optimization_barrier(jnp.sum(exponent, axis=-1, keepdims=True))

def newton_inverse(matrix):
    order_size = matrix.shape[-1]
    identity = jnp.eye(order_size, dtype=matrix.dtype)
    row_most = lax.optimization_barrier(jnp.max(lax.optimization_barrier(jnp.sum(matrix, axis=2)), axis=1))
    col_most = lax.optimization_barrier(jnp.max(lax.optimization_barrier(jnp.sum(matrix, axis=1)), axis=1))
    iterate = jnp.swapaxes(matrix, 1, 2) / (row_most * col_most)[:, None, None]
    for sweep_index in range(ITERS):
        product = contract_product('hij,hjk->hik', matrix, iterate)
        inner_term = contract_product('hij,hjk->hik', product, 7.0 * identity - product)
        outer_term = contract_product('hij,hjk->hik', product, 15.0 * identity - inner_term)
        iterate = 0.25 * contract_product('hij,hjk->hik', iterate, 13.0 * identity - outer_term)
    return iterate

def split_heads(matrix):
    return matrix.reshape(matrix.shape[0], HEAD_TOTAL, HEAD_FEATURES)

def landmark_means(matrix):
    return matrix.reshape(M, SEQUENCE_LENGTH // M, HEAD_TOTAL * HEAD_FEATURES).mean(axis=1)

def depthwise(values, kernel):
    half_span = (KS - 1) // 2
    padded = jnp.pad(values, ((half_span, half_span), (0, 0)))
    channel_taps = jnp.repeat(kernel, HEAD_FEATURES, axis=0)
    result = jnp.zeros_like(values)
    for offset in range(KS):
        result = result + channel_taps[:, offset] * padded[offset:offset + SEQUENCE_LENGTH]
    return result

def forward(queries, keys, values, kernel):
    scale_multiplier = HEAD_FEATURES ** (-0.5)
    query_per_head = split_heads(queries)
    key_per_head = split_heads(keys)
    value_per_head = split_heads(values)
    landmark_query_rows = split_heads(landmark_means(queries))
    landmark_key_rows = split_heads(landmark_means(keys))
    nearby_weight = row_softmax(contract_product('ckr,akr->kca', query_per_head, landmark_key_rows) * scale_multiplier)
    central_kernel = row_softmax(contract_product('bog,sog->obs', landmark_query_rows, landmark_key_rows) * scale_multiplier)
    distant_weight = row_softmax(contract_product('guf,juf->ugj', landmark_query_rows, key_per_head) * scale_multiplier)
    value_summary = contract_product('pgf,fps->pgs', distant_weight, value_per_head)
    pseudo_inverse = newton_inverse(central_kernel)
    weighted_values = contract_product('wej,wjy->wey', pseudo_inverse, value_summary)
    attention_output = contract_product('bvr,bre->vbe', nearby_weight, weighted_values).reshape(SEQUENCE_LENGTH, HEAD_TOTAL * HEAD_FEATURES)
    return attention_output + depthwise(values, kernel)

def reference(queries, keys, values, kernel, cotangent):

    def one_sequence(sequence_items):
        mixed, pullback = jax.vjp(forward, sequence_items[0], sequence_items[1], sequence_items[2], kernel)
        gradients = pullback(sequence_items[3])
        return (mixed, gradients[0], gradients[1], gradients[2], gradients[3])
    mixed, query_grad, key_grad, value_grad, kernel_parts = lax.map(one_sequence, (queries, keys, values, cotangent))
    kernel_grad = lax.optimization_barrier(jnp.sum(kernel_parts, axis=0)) / math.sqrt(BATCH * SEQUENCE_LENGTH * HEAD_FEATURES)
    return (mixed, query_grad, key_grad, value_grad, kernel_grad)
```

```python
import math

import jax
import jax.numpy as jnp
from jax import lax
from jax.experimental import pallas as pl
from jax.experimental.pallas import tpu as pltpu
from jax.sharding import PartitionSpec as P

F = 128
M = 128
SEGMENT = 64
NY, NZ = 4, 8
CHIPS = NY * NZ
HEADS = 8
ROWS = 256
HALF = 128
WIDE = HEADS * F
TAPS = 33
HALO = 16
PIECE = 72
QUARTER = 32
SCALE = F ** (-0.5)
f32, bf16 = jnp.float32, jnp.bfloat16


def split(x):
    high = x.astype(bf16)
    return high, (x - high.astype(f32)).astype(bf16)


def mm(a, b, ca, cb):
    return lax.dot_general(a, b, (((ca,), (cb,)), ((), ())), preferred_element_type=f32)


def mm3(a, b, ca, cb):
    return mm(a[0], b[0], ca, cb) + (mm(a[0], b[1], ca, cb) + mm(a[1], b[0], ca, cb))


def mmf(a, b, ca, cb):
    return lax.dot_general(
        a, b, (((ca,), (cb,)), ((), ())), preferred_element_type=f32, precision=lax.Precision.HIGHEST
    )


def remote(src, dst, send, recv, ctx, batch=None):
    where = {"ctx": ctx} if batch is None else {"ctx": ctx, "batch": batch}
    return pltpu.make_async_remote_copy(
        src_ref=src, dst_ref=dst, send_sem=send, recv_sem=recv, device_id=where,
        device_id_type=pl.DeviceIdType.MESH,
    )


def offset(i):
    return (2 * (i % 2) - 1) * ((i + 1) // 2)


def kernel(
    q, k, v, g, taps,
    mixed_o, dq_o, dk_o, dv_o, marks_o, kg_o,
    Qs, Ks, Vs, Gs, marks, qm_s, km_s, N_s, E_s, st_s, kgp, mixed_s, dq_s, dk_s, dv_s,
    parts, bufA, bufB, in_lo, in_hi, red, zbuf, W3, fix, out4, bufA4, bufB4, lo4, hi4, red4, zbuf4, fin, kgb,
    in_sem, xs, xr, hs, hr, ag1, ag3, rs2s, rs2r, rs2zs, rs2zr, rs4s, rs4r, rs4zs, rs4zr,
    os_l, os_s, os_r, kgs, kgr,
):
    me = lax.axis_index("ctx")
    x = lax.axis_index("batch")
    core = me % 2
    chip = me // 2
    y = chip // NZ
    z = chip % NZ
    yp, ym, y2 = (y + 1) % NY, (y + NY - 1) % NY, (y + 2) % NY
    sib = chip * 2 + (1 - core)

    def dev(yy, zz):
        return (yy * NZ + zz) * 2 + core

    nxt, prv = ((chip + 1) % CHIPS) * 2 + core, ((chip + CHIPS - 1) % CHIPS) * 2 + core

    barrier = pltpu.get_barrier_semaphore()

    def greet(ctx, batch=None):
        where = {"ctx": ctx} if batch is None else {"ctx": ctx, "batch": batch}
        pl.semaphore_signal(barrier, inc=1, device_id=where, device_id_type=pl.DeviceIdType.MESH)

    for d in range(1, NZ):
        greet(dev(y, (z + d) % NZ))
    for other in (dev(yp, z), dev(ym, z), nxt, prv):
        greet(other)
    for dx in range(4):
        for dc in range(2):
            if dx + dc:
                greet(chip * 2 + (core + dc) % 2, (x + dx) % 4)

    mine = pl.ds(pl.multiple_of(core * WIDE, F), WIDE)
    theirs = pl.ds(pl.multiple_of((1 - core) * WIDE, F), WIDE)
    sources = (q, k, v, g)
    targets = (Qs, Ks, Vs, Gs)
    bases = (0, 0, HALO, HALO)

    def rows_of(base, c):
        return pl.ds(pl.multiple_of(base + c * HALF, 8), HALF)

    own_in = [
        pltpu.make_async_copy(s.at[:, mine], t.at[rows_of(b, core)], in_sem.at[i])
        for i, (s, t, b) in enumerate(zip(sources, targets, bases))
    ]
    for c in own_in:
        c.start()
    pl.semaphore_wait(barrier, NZ - 1 + 4 + 7)
    sib_in = [
        remote(s.at[:, theirs], t.at[rows_of(b, core)], xs.at[i], xr.at[i], sib)
        for i, (s, t, b) in enumerate(zip(sources, targets, bases))
    ]
    sib_out = [
        remote(s.at[:, theirs], t.at[rows_of(b, 1 - core)], xs.at[i], xr.at[i], sib)
        for i, (s, t, b) in enumerate(zip(sources, targets, bases))
    ]
    for c in sib_in:
        c.start()
    Vs[HALO + ROWS + HALO:, :] = jnp.zeros((3 * HALF - ROWS - 2 * HALO, WIDE), f32)

    for i in (0, 1):
        own_in[i].wait()
        sib_out[i].wait_recv()

    def mark(h, carry):
        lanes = pl.ds(pl.multiple_of(h * F, F), F)
        a = jnp.sum(Qs[:, lanes].reshape(4, SEGMENT, F), axis=1)
        b = jnp.sum(Ks[:, lanes].reshape(4, SEGMENT, F), axis=1)
        marks[chip, h] = jnp.concatenate([a, b], axis=0) * (1.0 / SEGMENT)
        return carry

    lax.fori_loop(0, HEADS, mark, 0)

    def gather(buf, na, nb, sems):
        zs, zr, ps, pr, ms, mr, as_, ar, bs, br = [sems.at[i] for i in range(10)]
        first, second = pl.ds(0, na), pl.ds(na, nb)

        def to_z(zz):
            return remote(buf.at[chip], buf.at[chip], zs.at[zz], zr.at[z], dev(y, zz))

        def from_z(zz):
            p = y * NZ + zz
            return remote(buf.at[p], buf.at[p], zs.at[zz], zr.at[zz], dev(y, zz))

        def up(zz, yy):
            p = yy * NZ + zz
            return remote(buf.at[p], buf.at[p], ps.at[zz], pr.at[zz], dev(yp, z))

        def down(zz, yy):
            p = yy * NZ + zz
            return remote(buf.at[p], buf.at[p], ms.at[zz], mr.at[zz], dev(ym, z))

        def up_half(zz, yy):
            p = yy * NZ + zz
            return remote(buf.at[p, first], buf.at[p, first], as_.at[zz], ar.at[zz], dev(yp, z))

        def down_half(zz, yy):
            p = yy * NZ + zz
            return remote(buf.at[p, second], buf.at[p, second], bs.at[zz], br.at[zz], dev(ym, z))

        def forward(zz):
            up(zz, y).start()
            down(zz, y).start()

        def half(zz):
            up(zz, ym).wait_recv()
            up_half(zz, ym).start()
            down(zz, yp).wait_recv()
            down_half(zz, yp).start()

        def at(i):
            return (z + NZ + offset(i)) % NZ

        def start():
            for i in range(1, NZ):
                to_z(at(i)).start()
            forward(z)

        def step(i):
            zz = at(i)
            from_z(zz).wait_recv()
            forward(zz)

        def half_step(i):
            half(at(i))

        def finish():
            def one(zz, carry):
                up_half(zz, y2).wait_recv()
                down_half(zz, y2).wait_recv()
                return carry

            lax.fori_loop(0, NZ, one, 0)

        def drain():
            def one(zz, carry):
                up(zz, y).wait_send()
                down(zz, y).wait_send()
                up_half(zz, ym).wait_send()
                down_half(zz, yp).wait_send()
                return carry

            lax.fori_loop(0, NZ, one, 0)
            for i in range(1, NZ):
                to_z(at(i)).wait_send()

        return start, step, half_step, finish, drain

    start1, step1, half1, finish1, drain1 = gather(marks, 4, 4, ag1)
    start1()

    for i in (2, 3):
        own_in[i].wait()
        sib_out[i].wait_recv()
    last, low = pl.ds(ROWS, HALO), pl.ds(0, HALO)
    lead, high = pl.ds(HALO, HALO), pl.ds(HALO + ROWS, HALO)
    halos = []
    for i, t in enumerate((Vs, Gs)):
        halos.append(remote(t.at[last], t.at[low], hs.at[2 * i], hr.at[2 * i], nxt))
        halos.append(remote(t.at[lead], t.at[high], hs.at[2 * i + 1], hr.at[2 * i + 1], prv))
    for c in halos:
        c.start()
    step1(1)
    step1(2)
    half1(0)
    for c in halos:
        c.wait_recv()

    @pl.when(chip == 0)
    def _():
        Vs[0:HALO, :] = jnp.zeros((HALO, WIDE), f32)
        Gs[0:HALO, :] = jnp.zeros((HALO, WIDE), f32)

    @pl.when(chip == CHIPS - 1)
    def _():
        Vs[HALO + ROWS:HALO + ROWS + HALO, :] = jnp.zeros((HALO, WIDE), f32)
        Gs[HALO + ROWS:HALO + ROWS + HALO, :] = jnp.zeros((HALO, WIDE), f32)

    def convolve(h):
        lanes = pl.ds(pl.multiple_of(h * F, F), F)
        ahead = jnp.broadcast_to(taps[pl.ds(core * HEADS + h, 1), :], (HALF, 2 * HALF))
        back = jnp.broadcast_to(taps[pl.ds((2 + core) * HEADS + h, 1), :], (HALF, 2 * HALF))
        ahead = split(pltpu.roll(ahead, 0, 1, stride=1, stride_axis=0)[:, : HALF + 2 * HALO])
        back = split(pltpu.roll(back, 0, 1, stride=1, stride_axis=0)[:, : HALF + 2 * HALO])
        total = jnp.zeros((HALF, 2 * HALF), f32)
        for b in range(2):
            window = pl.ds(b * HALF, HALF + 2 * HALO)
            vw = split(Vs[pl.ds(b * HALF, 2 * HALF), lanes])
            near_v = (vw[0][: HALF + 2 * HALO], vw[1][: HALF + 2 * HALO])
            mixed_s[pl.ds(b * HALF, HALF), lanes] = mm3(ahead, near_v, 1, 0)
            dv_s[pl.ds(b * HALF, HALF), lanes] = mm3(back, split(Gs[window, lanes]), 1, 0)
            total = total + mm3(split(Gs[pl.ds(HALO + b * HALF, HALF), lanes]), vw, 1, 1)
        acc = total[:8]
        for block in range(1, HALF // 8):
            acc = acc + pltpu.roll(total[block * 8:(block + 1) * 8], 2 * HALF - 8 * block, 1)
        line = acc[:1]
        for r in range(1, 8):
            line = line + pltpu.roll(acc[r:r + 1], 2 * HALF - r, 1)
        kgp[h] = jnp.broadcast_to(line[:, :F], (8, F))

    for i in range(3, NZ):
        step1(i)
        half1(i - 2)
        convolve(jnp.int32(i - 3))
    half1(NZ - 2)
    half1(NZ - 1)
    for i in range(NZ - 3, HEADS):
        convolve(jnp.int32(i))
    finish1()

    low_rows = lax.broadcasted_iota(jnp.int32, (CHIPS // 2, 8, F), 1) < 4

    def landmarks(h):
        t = marks[:, pl.ds(h, 1)].reshape(2 * M, F)
        r = pltpu.roll(t, 2 * M - 4, 0).reshape(CHIPS // 2, 2, 8, F)
        t = t.reshape(CHIPS // 2, 2, 8, F)
        qm = jnp.where(low_rows, t[:, 0], r[:, 0]).reshape(M, F)
        km = jnp.where(low_rows, r[:, 0], t[:, 1]).reshape(M, F)
        return qm, km

    def combine(pieces):
        tops = [p[2 * QUARTER:2 * QUARTER + 1] for p in pieces]
        top = tops[0]
        for t in tops[1:]:
            top = jnp.maximum(top, t)
        sums, rest, totals, grads = 0.0, 0.0, 0.0, 0.0
        for p, t in zip(pieces, tops):
            factor = jnp.exp(t - top)
            sums = sums + p[:QUARTER] * factor
            rest = rest + p[QUARTER:2 * QUARTER]
            totals = totals + p[2 * QUARTER + 1:2 * QUARTER + 2] * factor
            grads = grads + p[2 * QUARTER + 2:2 * QUARTER + 3]
        return sums, rest, top, totals, grads

    def stats(*rows):
        return jnp.concatenate(list(rows) + [jnp.zeros((8 - len(rows), M), f32)], axis=0)

    def put(ref, index, sums, rest, tile):
        ref[index, 0:QUARTER] = sums
        ref[index, QUARTER:2 * QUARTER] = rest
        ref[index, 2 * QUARTER:PIECE] = tile

    def forward_head(h):
        lanes = pl.ds(pl.multiple_of(h * F, F), F)
        qm, km = landmarks(h)
        qm_s[h] = qm
        km_s[h] = km
        scores = mm3(split(Qs[:, lanes]), split(km), 1, 1) * SCALE
        e = jnp.exp(scores - jnp.max(scores, axis=-1, keepdims=True))
        near = e / jnp.sum(e, axis=-1, keepdims=True)
        N_s[h] = near
        scores = mm3(split(Ks[:, lanes]), split(qm), 1, 1) * SCALE
        top = jnp.max(scores, axis=0, keepdims=True)
        e = jnp.exp(scores - top)
        E_s[h] = e
        own = pl.ds(HALO, ROWS)
        summary = mm3(split(Vs[own, lanes]), split(e), 0, 0)
        grad = mm3(split(Gs[own, lanes]), split(near), 0, 0)
        tile = stats(top, jnp.sum(e, axis=0, keepdims=True), kgp[h][0:1])
        st_s[h] = tile
        for p in range(4):
            put(parts, h * 4 + p, summary[p * QUARTER:(p + 1) * QUARTER], grad[p * QUARTER:(p + 1) * QUARTER], tile)

    def four(ref, first):
        return ref.at[pl.ds(first, 4)]

    def head_of(yy, j):
        return 4 * (2 * yy + j)

    send2 = [
        remote(four(parts, head_of(y2, 0)), bufA, rs2s.at[0], rs2r.at[0], dev(yp, z)),
        remote(four(parts, head_of(y2, 1)), bufB, rs2s.at[1], rs2r.at[1], dev(ym, z)),
        remote(four(parts, head_of(yp, 0)), in_lo.at[0], rs2s.at[2], rs2r.at[2], dev(yp, z)),
        remote(four(parts, head_of(yp, 1)), in_lo.at[1], rs2s.at[3], rs2r.at[3], dev(yp, z)),
        remote(four(parts, head_of(ym, 0)), in_hi.at[0], rs2s.at[4], rs2r.at[4], dev(ym, z)),
        remote(four(parts, head_of(ym, 1)), in_hi.at[1], rs2s.at[5], rs2r.at[5], dev(ym, z)),
    ]

    def fold(first, buf):
        def one(p, carry):
            sums, rest, top, totals, grads = combine([parts[first + p], buf[p]])
            put(parts, first + p, sums, rest, stats(top, totals, grads))
            return carry

        lax.fori_loop(0, 4, one, 0)

    def forward_step(i, carry):
        n = i // 2
        turn = jnp.where(n == 0, 2, jnp.where(n == 1, 1, jnp.where(n == 2, 3, 0)))
        forward_head(2 * ((y + turn) % NY) + i % 2)

        @pl.when(i == 0)
        def _():
            send2[0].start()

        @pl.when(i == 1)
        def _():
            send2[1].start()

        @pl.when(i == 2)
        def _():
            send2[0].wait_recv()
            fold(head_of(yp, 0), bufA)
            send2[2].start()

        @pl.when(i == 3)
        def _():
            send2[3].start()

        @pl.when(i == 4)
        def _():
            send2[4].start()

        @pl.when(i == 5)
        def _():
            send2[1].wait_recv()
            fold(head_of(ym, 1), bufB)
            send2[5].start()

        return carry

    lax.fori_loop(0, HEADS, forward_step, 0)

    served = chip // 4
    qm, km = qm_s[served], km_s[served]
    scores = mmf(qm, km, 1, 1) * SCALE
    e = jnp.exp(scores - jnp.max(scores, axis=-1, keepdims=True))
    A = e / jnp.sum(e, axis=-1, keepdims=True)
    eye = (
        lax.broadcasted_iota(jnp.int32, (M, M), 0) == lax.broadcasted_iota(jnp.int32, (M, M), 1)
    ).astype(f32)
    row_sum = jnp.sum(A, axis=1, keepdims=True)
    col_sum = jnp.sum(A, axis=0, keepdims=True)
    row_most = jnp.max(row_sum, axis=0, keepdims=True)
    col_most = jnp.max(col_sum, axis=1, keepdims=True)
    shrink = 1.0 / (row_most * col_most)
    Z = A.T * shrink
    trail = []

    def newton(Z):
        Pm = mmf(A, Z, 1, 0)
        H = 7.0 * eye - Pm
        E = 15.0 * eye - mmf(Pm, H, 1, 0)
        C = 13.0 * eye - mmf(Pm, E, 1, 0)
        trail.append((Z, Pm, H, E, C))
        return 0.25 * mmf(Z, C, 1, 0)

    def to_z2(zz):
        return remote(red.at[zz], zbuf.at[z], rs2zs.at[zz], rs2zr.at[z], dev(y, zz))

    def from_z2(zz):
        return remote(red.at[zz], zbuf.at[zz], rs2zs.at[zz], rs2zr.at[zz], dev(y, zz))

    def settle(j):
        send2[2 + j].wait_recv()
        send2[4 + j].wait_recv()

        def one(p, carry):
            zz = 4 * j + p
            sums, rest, top, totals, grads = combine([parts[8 * y + zz], in_lo[j, p], in_hi[j, p]])
            put(red, zz, sums, rest, stats(top, totals, grads))

            @pl.when(zz != z)
            def _():
                to_z2(zz).start()

            @pl.when(zz == z)
            def _():
                zbuf[zz] = red[zz]

            return carry

        lax.fori_loop(0, 4, one, 0)

    Z = newton(Z)
    settle(0)
    Z = newton(Z)
    settle(1)
    Z = newton(Z)
    for d in range(1, NZ):
        from_z2((z + d) % NZ).wait_recv()
    sums, weight_grad, top, totals, grads = combine([zbuf[i] for i in range(NZ)])
    summary = sums / totals
    weighted = mmf(summary, Z, 1, 1)
    summary_grad = mmf(weight_grad, Z, 1, 0)
    put(
        W3, chip, weighted, summary_grad,
        stats(top, totals, jnp.sum(summary_grad * summary, axis=0, keepdims=True), grads),
    )
    start3, step3, half3, finish3, drain3 = gather(W3, 40, 32, ag3)
    start3()

    dZ = mmf(weight_grad, summary, 0, 0)
    dA = jnp.zeros((M, M), f32)
    at_step = 1
    for Zi, Pm, H, E, C in reversed(trail):
        dC = 0.25 * mmf(Zi, dZ, 0, 0)
        dZ = 0.25 * mmf(dZ, C, 1, 1)
        step3(at_step)
        dP = -mmf(dC, E, 1, 1)
        dE = -mmf(Pm, dC, 0, 0)
        if at_step > 1:
            half3(at_step - 2)
        dP = dP - mmf(dE, H, 1, 1)
        dH = -mmf(Pm, dE, 0, 0)
        dP = dP - dH
        step3(at_step + 1)
        dA = dA + mmf(dP, Zi, 1, 1)
        dZ = dZ + mmf(A, dP, 0, 0)
        half3(at_step - 1)
        at_step += 2
    step3(7)
    half3(5)
    half3(6)
    half3(7)
    dA = dA + (dZ * shrink).T
    shrink_grad = jnp.sum(jnp.sum(dZ * A.T, axis=1, keepdims=True), axis=0, keepdims=True)
    product_grad = -shrink_grad * shrink * shrink
    row_hit = (row_sum == row_most).astype(f32)
    col_hit = (col_sum == col_most).astype(f32)
    dA = dA + product_grad * col_most * row_hit / jnp.sum(row_hit, axis=0, keepdims=True)
    dA = dA + product_grad * row_most * col_hit / jnp.sum(col_hit, axis=1, keepdims=True)
    middle = A * (dA - jnp.sum(dA * A, axis=-1, keepdims=True)) * SCALE
    fix[0] = mmf(middle, km, 1, 0)
    fix[1] = mmf(middle, qm, 0, 0)
    finish3()

    kgb[core, x] = jnp.concatenate([W3[4 * h, 2 * QUARTER + 3:2 * QUARTER + 4] for h in range(HEADS)], axis=0)
    taps_out = []
    for dx in range(4):
        for dc in range(2):
            if dx + dc:
                xx, cc = (x + dx) % 4, (core + dc) % 2
                i = dx * 2 + dc
                taps_out.append((
                    remote(kgb.at[core, x], kgb.at[core, x], kgs.at[i], kgr.at[core, x], chip * 2 + cc, xx),
                    remote(kgb.at[cc, xx], kgb.at[cc, xx], kgs.at[i], kgr.at[cc, xx], chip * 2 + cc, xx),
                ))
    for c, _ in taps_out:
        c.start()

    def scattered(a, b):
        first = jnp.where(low_rows, a.reshape(CHIPS // 2, 8, F), pltpu.roll(b, 4, 0).reshape(CHIPS // 2, 8, F))
        second = jnp.where(low_rows, pltpu.roll(a, M - 4, 0).reshape(CHIPS // 2, 8, F), b.reshape(CHIPS // 2, 8, F))
        return first, second

    def backward_head(h):
        lanes = pl.ds(pl.multiple_of(h * F, F), F)
        own = pl.ds(HALO, ROWS)
        got = W3[pl.ds(4 * h, 4)]
        wt = split(got[:, :QUARTER].reshape(F, M))
        st = split(got[:, QUARTER:2 * QUARTER].reshape(F, M))
        top = got[0, 2 * QUARTER:2 * QUARTER + 1]
        totals = got[0, 2 * QUARTER + 1:2 * QUARTER + 2]
        fdot = jnp.sum(got[:, 2 * QUARTER + 2], axis=0, keepdims=True)
        near = N_s[h]
        gs = split(Gs[own, lanes])
        mixed_s[:, lanes] = mixed_s[:, lanes] + mm3(split(near), wt, 1, 1)
        dn = mm3(gs, wt, 1, 0)
        ns = split(near * (dn - jnp.sum(dn * near, axis=-1, keepdims=True)) * SCALE)
        dq_s[:, lanes] = mm3(ns, split(km_s[h]), 1, 0)
        dkm = mm3(ns, split(Qs[:, lanes]), 0, 0)
        far = E_s[h] * (jnp.exp(st_s[h][0:1] - top) / totals)
        dv_s[:, lanes] = dv_s[:, lanes] + mm3(split(far), st, 1, 1)
        df = mm3(split(Vs[own, lanes]), st, 1, 0)
        fs = split(far * (df - fdot) * SCALE)
        dk_s[:, lanes] = mm3(fs, split(qm_s[h]), 1, 0)
        dqm = mm3(fs, split(Ks[:, lanes]), 0, 0)
        share = (h == served).astype(f32)
        first, second = scattered(dqm + share * fix[0], dkm + share * fix[1])
        both = jnp.stack([first, second], axis=1).reshape(CHIPS, 8, F)
        out4[h] = both

    def blocks(h, yy):
        return out4.at[h, pl.ds(yy * NZ, NZ)]

    def far4(h, up):
        if up:
            return remote(blocks(h, y2), bufA4.at[h // 2], rs4s.at[0, h], rs4r.at[0, h], dev(yp, z))
        return remote(blocks(h, y2), bufB4.at[h // 2], rs4s.at[0, h], rs4r.at[0, h], dev(ym, z))

    def up4(h):
        return remote(blocks(h, yp), lo4.at[h], rs4s.at[1, h], rs4r.at[1, h], dev(yp, z))

    def down4(h):
        return remote(blocks(h, ym), hi4.at[h], rs4s.at[2, h], rs4r.at[2, h], dev(ym, z))

    def backward_step(i, carry):
        n = i // 2
        turn = jnp.where(n == 0, 0, jnp.where(n == 1, 1, jnp.where(n == 2, 3, 2)))
        h = 2 * ((y + turn) % NY) + i % 2
        backward_head(h)

        @pl.when(i % 2 == 0)
        def _():
            far4(h, True).start()
            down4(h).start()

        @pl.when(i % 2 == 1)
        def _():
            far4(h, False).start()
            up4(h).start()

        return carry

    lax.fori_loop(0, HEADS, backward_step, 0)

    outs = []
    for i, (s, t) in enumerate(((mixed_s, mixed_o), (dv_s, dv_o), (dq_s, dq_o), (dk_s, dk_o))):
        outs.append((
            pltpu.make_async_copy(s.at[rows_of(0, core)], t.at[:, mine], os_l.at[i]),
            remote(s.at[rows_of(0, 1 - core)], t.at[:, mine], os_s.at[i], os_r.at[i], sib),
            remote(s.at[rows_of(0, 1 - core)], t.at[:, theirs], os_s.at[i], os_r.at[i], sib),
        ))
    for a, b, _ in outs:
        a.start()
        b.start()

    def relay(n, carry):
        even, odd = 2 * n, 2 * n + 1
        far4(even, True).wait_recv()
        mid = pl.ds(yp * NZ, NZ)
        out4[even, mid] = out4[even, mid] + bufA4[n]
        up4(even).start()
        far4(odd, False).wait_recv()
        mid = pl.ds(ym * NZ, NZ)
        out4[odd, mid] = out4[odd, mid] + bufB4[n]
        down4(odd).start()
        return carry

    lax.fori_loop(0, HEADS // 2, relay, 0)

    def meet(h, carry):
        up4(h).wait_recv()
        down4(h).wait_recv()
        here = out4[h, pl.ds(y * NZ, NZ)] + lo4[h] + hi4[h]
        for zz in range(NZ):
            red4[zz, h] = here[zz]
        return carry

    lax.fori_loop(0, HEADS, meet, 0)

    def to_z4(zz):
        return remote(red4.at[zz], zbuf4.at[z], rs4zs.at[zz], rs4zr.at[z], dev(y, zz))

    def from_z4(zz):
        return remote(red4.at[zz], zbuf4.at[zz], rs4zs.at[zz], rs4zr.at[zz], dev(y, zz))

    for i in range(1, NZ):
        to_z4((z + NZ + offset(i)) % NZ).start()
    zbuf4[z] = red4[z]
    for _, c in taps_out:
        c.wait_recv()
    kg_o[...] = jnp.concatenate([kgb[c, 0] + kgb[c, 1] + kgb[c, 2] + kgb[c, 3] for c in range(2)], axis=0)
    for i in range(1, NZ):
        from_z4((z + NZ + offset(i)) % NZ).wait_recv()
    for h in range(HEADS):
        total = zbuf4[0, h]
        for i in range(1, NZ):
            total = total + zbuf4[i, h]
        fin[:, h * F:(h + 1) * F] = total * (1.0 / SEGMENT)
    marks_out = (
        pltpu.make_async_copy(fin, marks_o.at[:, mine], os_l.at[4]),
        remote(fin, marks_o.at[:, mine], os_s.at[4], os_r.at[4], sib),
        remote(fin, marks_o.at[:, theirs], os_s.at[4], os_r.at[4], sib),
    )
    marks_out[0].start()
    marks_out[1].start()
    outs.append(marks_out)

    for c in sib_in:
        c.wait_send()
    for c in halos:
        c.wait_send()
    drain1()
    drain3()
    for c in send2:
        c.wait_send()
    for d in range(1, NZ):
        to_z2((z + d) % NZ).wait_send()
        to_z4((z + d) % NZ).wait_send()

    def ends(n, carry):
        far4(2 * n, True).wait_send()
        far4(2 * n + 1, False).wait_send()
        for h in (2 * n, 2 * n + 1):
            up4(h).wait_send()
            down4(h).wait_send()
        return carry

    lax.fori_loop(0, HEADS // 2, ends, 0)
    for c, _ in taps_out:
        c.wait_send()
    for a, b, c in outs:
        a.wait()
        b.wait_send()
        c.wait_recv()


def layer(queries, keys, values, kernel_taps, cotangent):
    head_total = kernel_taps.shape[0]
    table = jnp.concatenate([kernel_taps, kernel_taps[:, ::-1]], axis=0)
    table = jnp.pad(table, ((0, 0), (0, 2 * HALF - TAPS)))
    rows, wide = queries.shape[1:]
    DMA = pltpu.SemaphoreType.DMA

    def vm(*shape):
        return pltpu.VMEM(shape, f32)

    anywhere = pl.BlockSpec(memory_space=pl.ANY)
    vmem = pl.BlockSpec(memory_space=pltpu.VMEM)
    big = jax.ShapeDtypeStruct((rows, wide), f32)
    outs = pl.pallas_call(
        kernel,
        out_shape=(big, big, big, big, jax.ShapeDtypeStruct((8, wide), f32), jax.ShapeDtypeStruct((2 * HEADS, F), f32)),
        in_specs=[anywhere] * 4 + [vmem],
        out_specs=(anywhere,) * 5 + (vmem,),
        scratch_shapes=[
            vm(ROWS, WIDE), vm(ROWS, WIDE), vm(3 * HALF, WIDE), vm(ROWS + 2 * HALO, WIDE),
            vm(CHIPS, HEADS, 8, F), vm(HEADS, M, F), vm(HEADS, M, F), vm(HEADS, ROWS, M), vm(HEADS, ROWS, M),
            vm(HEADS, 8, M), vm(HEADS, 8, F), vm(ROWS, WIDE), vm(ROWS, WIDE), vm(ROWS, WIDE), vm(ROWS, WIDE),
            vm(CHIPS, PIECE, M), vm(4, PIECE, M), vm(4, PIECE, M), vm(2, 4, PIECE, M), vm(2, 4, PIECE, M),
            vm(NZ, PIECE, M), vm(NZ, PIECE, M), vm(CHIPS, PIECE, M), vm(2, M, F),
            vm(HEADS, CHIPS, 8, F), vm(HEADS // 2, NZ, 8, F), vm(HEADS // 2, NZ, 8, F),
            vm(HEADS, NZ, 8, F), vm(HEADS, NZ, 8, F), vm(NZ, HEADS, 8, F), vm(NZ, HEADS, 8, F), vm(8, WIDE),
            vm(2, 4, HEADS, F),
            DMA((4,)), DMA((4,)), DMA((4,)), DMA((4,)), DMA((4,)), DMA((10, NZ)), DMA((10, NZ)),
            DMA((6,)), DMA((6,)), DMA((NZ,)), DMA((NZ,)), DMA((3, HEADS)), DMA((3, HEADS)), DMA((NZ,)), DMA((NZ,)),
            DMA((5,)), DMA((5,)), DMA((5,)), DMA((8,)), DMA((2, 4)),
        ],
        compiler_params=pltpu.CompilerParams(
            collective_id=0, has_side_effects=True, vmem_limit_bytes=48 * 1024 * 1024
        ),
    )(queries[0], keys[0], values[0], cotangent[0], table)
    mixed, dq, dk, dv, marks, taps_grad = outs
    core = lax.axis_index("ctx") % 2
    own = rows // SEGMENT

    def spread(first):
        picked = lax.dynamic_slice_in_dim(marks, first + core * own, own, 0)
        return jnp.broadcast_to(picked[:, None, :], (own, SEGMENT, wide)).reshape(rows, wide)

    total = lax.axis_size("batch") * lax.axis_size("ctx") * rows * F
    taps_grad = taps_grad[:, :TAPS] / math.sqrt(total)
    return mixed[None], (dq + spread(0))[None], (dk + spread(4))[None], dv[None], taps_grad


def solution(mesh):
    block = P("batch", "ctx", None)
    return jax.shard_map(
        layer, mesh=mesh, in_specs=(block, block, block, P(), block),
        out_specs=(block, block, block, block, P()), check_vma=False,
    )
```

```python
import functools
import math

import jax
import jax.numpy as jnp
from jax import lax
from jax.experimental import pallas as pl
from jax.experimental.pallas import tpu as pltpu
from jax.sharding import PartitionSpec as P

F = 128
M = 128
SEGMENT = 64
NY, NZ = 4, 8
CHIPS = NY * NZ
HEADS = 8
HALF_HEADS = 4
ROWS = 256
HALF = 128
WIDE = HEADS * F
TAPS = 33
HALO = 16
PIECE = 72
QUARTER = 32
SCALE = F ** (-0.5)
f32, bf16 = jnp.float32, jnp.bfloat16


def split(x):
    high = x.astype(bf16)
    return high, (x - high.astype(f32)).astype(bf16)


def mm(a, b, ca, cb):
    return lax.dot_general(a, b, (((ca,), (cb,)), ((), ())), preferred_element_type=f32)


def mm3(a, b, ca, cb):
    return mm(a[0], b[0], ca, cb) + (mm(a[0], b[1], ca, cb) + mm(a[1], b[0], ca, cb))


def mmf(a, b, ca, cb):
    return lax.dot_general(
        a, b, (((ca,), (cb,)), ((), ())), preferred_element_type=f32, precision=lax.Precision.HIGHEST
    )


def remote(src, dst, send, recv, ctx, batch=None):
    where = {"ctx": ctx} if batch is None else {"ctx": ctx, "batch": batch}
    return pltpu.make_async_remote_copy(
        src_ref=src, dst_ref=dst, send_sem=send, recv_sem=recv, device_id=where,
        device_id_type=pl.DeviceIdType.MESH,
    )


def offset(i):
    return (2 * (i % 2) - 1) * ((i + 1) // 2)


def kernel(
    q, k, v, g, taps_in,
    mixed_o, dq_o, dk_o, dv_o, marks_o, kg_o,
    Qf, Kf, own_marks, sib_marks, tap_raw, taps, Qs, Ks, Vs, Gs, marks, qm_s, km_s, N_s, E_s, st_s, kgp, mixed_s, dq_s, dk_s, dv_s,
    parts, from_rows, red, zbuf, W3, served_s, fix, out4, buf4, red4, zbuf4, fin,
    kgz, kgy, kgb,
    in_sem, xs, xr, hs, hr, ag1, ag3, rs2s, rs2r, rs2zs, rs2zr, rs4s, rs4r, rs4zs, rs4zr,
    os_l, os_s, os_r, kzs, kzr, kys, kyr, kgs, kgr,
):
    me = lax.axis_index("ctx")
    x = lax.axis_index("batch")
    core = me % 2
    chip = me // 2
    y = chip // NZ
    z = chip % NZ
    yp, ym, y2 = (y + 1) % NY, (y + NY - 1) % NY, (y + 2) % NY
    sib = chip * 2 + (1 - core)

    def dev(yy, zz):
        return (yy * NZ + zz) * 2 + core

    nxt, prv = ((chip + 1) % CHIPS) * 2 + core, ((chip + CHIPS - 1) % CHIPS) * 2 + core

    barrier = pltpu.get_barrier_semaphore()

    def greet(ctx, batch=None):
        where = {"ctx": ctx} if batch is None else {"ctx": ctx, "batch": batch}
        pl.semaphore_signal(barrier, inc=1, device_id=where, device_id_type=pl.DeviceIdType.MESH)

    for d in range(1, NZ):
        greet(dev(y, (z + d) % NZ))
    for other in (dev(yp, z), dev(ym, z), dev(y2, z), nxt, prv):
        greet(other)
    for dx in range(4):
        for dc in range(2):
            if dx + dc:
                greet(chip * 2 + (core + dc) % 2, (x + dx) % 4)

    mine = pl.ds(pl.multiple_of(core * WIDE, F), WIDE)
    theirs = pl.ds(pl.multiple_of((1 - core) * WIDE, F), WIDE)
    sources = (q, k, v, g)
    targets = (Qs, Ks, Vs, Gs)
    bases = (0, 0, HALO, HALO)

    def rows_of(base, c):
        return pl.ds(pl.multiple_of(base + c * HALF, 8), HALF)

    own_in = [
        pltpu.make_async_copy(s.at[:, mine], t.at[rows_of(b, core)], in_sem.at[i])
        for i, (s, t, b) in enumerate(zip(sources, targets, bases))
    ]
    full_in = [pltpu.make_async_copy(s, t, in_sem.at[4 + i]) for i, (s, t) in enumerate(((q, Qf), (k, Kf)))]
    taps_copy = pltpu.make_async_copy(taps_in, tap_raw, in_sem.at[6])
    taps_copy.start()
    for c in full_in:
        c.start()
    for c in own_in:
        c.start()
    for c in full_in:
        c.wait()
    tile_row = lax.broadcasted_iota(jnp.int32, (8, F), 0)

    def mark(n, carry):
        lanes = pl.ds(pl.multiple_of(n * F, F), F)
        tile = jnp.zeros((8, F), f32)
        for i, t in enumerate((Qf, Kf)):
            for m in range(2):
                mean = jnp.sum(t[m * SEGMENT:(m + 1) * SEGMENT, lanes], axis=0, keepdims=True) * (1.0 / SEGMENT)
                tile = tile + jnp.where(tile_row == 4 * i + 2 * core + m, mean, 0.0)
        own_marks[n // HEADS, n % 2, (n % HEADS) // 2] = tile
        return carry

    lax.fori_loop(0, 2 * HEADS, mark, 0)
    pl.semaphore_wait(barrier, NZ - 1 + 5 + 7)
    sib_in = [
        remote(s.at[:, theirs], t.at[rows_of(b, core)], xs.at[i], xr.at[i], sib)
        for i, (s, t, b) in enumerate(zip(sources, targets, bases))
    ]
    sib_out = [
        remote(s.at[:, theirs], t.at[rows_of(b, 1 - core)], xs.at[i], xr.at[i], sib)
        for i, (s, t, b) in enumerate(zip(sources, targets, bases))
    ]
    mark_in = remote(own_marks.at[1 - core], sib_marks, xs.at[4], xr.at[4], sib)
    mark_in.start()
    Vs[HALO + ROWS + HALO:, :] = jnp.zeros((3 * HALF - ROWS - 2 * HALO, WIDE), f32)

    mark_in.wait_recv()
    for j in range(2):
        marks[j, chip] = own_marks[core, j] + sib_marks[j]

    def gather(buf, sems, sources, own):
        sends, recvs = sems.at[0], sems.at[1]

        def piece(yy, zz, to):
            p = yy * NZ + zz
            row = (to - yy + NY) % NY
            return remote(buf.at[p], buf.at[p], sends.at[row, zz], recvs.at[row, zz], dev(to, z))

        def to_z(zz):
            return remote(buf.at[chip], buf.at[chip], sends.at[0, zz], recvs.at[0, z], dev(y, zz))

        def from_z(zz):
            p = y * NZ + zz
            return remote(buf.at[p], buf.at[p], sends.at[0, zz], recvs.at[0, zz], dev(y, zz))

        def forward(zz):
            for to in (y2, yp, ym):
                piece(y, zz, to).start()

        def start():
            for i in range(1, NZ):
                to_z((z + NZ + offset(NZ - i)) % NZ).start()
            forward(z)

        def step(i):
            zz = sources[i]

            def go():
                from_z(zz).wait_recv()
                forward(zz)

            if own is None:
                if i:
                    go()
            else:
                pl.when(zz != z)(go)

        def finish():
            for zz in sources:
                for yy in (yp, ym, y2):
                    piece(yy, zz, y).wait_recv()

        def drain():
            for zz in sources:
                for to in (yp, ym, y2):
                    piece(y, zz, to).wait_send()

            def sent():
                for i in range(1, NZ):
                    to_z((z + NZ + offset(i)) % NZ).wait_send()

            if own is None:
                sent()
            else:
                pl.when(own)(sent)

        return start, step, finish, drain

    parity = z % 2
    every = [(z + NZ + offset(i)) % NZ for i in range(NZ)]
    start1, step1, finish1, drain1 = zip(
        *[gather(marks.at[j], ag1.at[j], every, None) for j in range(2)]
    )

    def some(j):
        same = parity == j
        return [
            (z + NZ + jnp.where(same, a, b)) % NZ for a, b in ((0, 1), (2, -1), (-2, 3), (4, -3))
        ]

    start3, step3, finish3, drain3 = zip(
        *[gather(W3, ag3.at[j], some(j), parity == j) for j in range(2)]
    )
    start1[0]()
    for c in sib_in:
        c.start()
    start1[1]()

    last, low = pl.ds(ROWS, HALO), pl.ds(0, HALO)
    lead, high = pl.ds(HALO, HALO), pl.ds(HALO + ROWS, HALO)
    halos = []
    for i, t in enumerate((Vs, Gs)):
        halos.append(remote(t.at[last], t.at[low], hs.at[2 * i], hr.at[2 * i], nxt))
        halos.append(remote(t.at[lead], t.at[high], hs.at[2 * i + 1], hr.at[2 * i + 1], prv))
    for i in range(1, NZ):
        step1[0](i)
    for i in range(4):
        own_in[i].wait()
        sib_out[i].wait_recv()
    for c in halos:
        c.start()
    for i in range(1, NZ):
        step1[1](i)
    finish1[0]()

    taps_copy.wait()
    taps[...] = jnp.zeros((4 * HEADS, 2 * HALF), f32)
    taps[pl.ds(0, 2 * HEADS), pl.ds(0, TAPS)] = tap_raw[...]
    turned = (
        lax.broadcasted_iota(jnp.int32, (F, F), 0) + lax.broadcasted_iota(jnp.int32, (F, F), 1) == TAPS - 1
    ).astype(f32)
    taps[pl.ds(2 * HEADS, 2 * HEADS), pl.ds(0, F)] = mmf(taps[pl.ds(0, 2 * HEADS), pl.ds(0, F)], turned, 1, 0)

    def meet_halos():
        for c in halos:
            c.wait_recv()

        @pl.when(chip == 0)
        def _():
            Vs[0:HALO, :] = jnp.zeros((HALO, WIDE), f32)
            Gs[0:HALO, :] = jnp.zeros((HALO, WIDE), f32)

        @pl.when(chip == CHIPS - 1)
        def _():
            Vs[HALO + ROWS:HALO + ROWS + HALO, :] = jnp.zeros((HALO, WIDE), f32)
            Gs[HALO + ROWS:HALO + ROWS + HALO, :] = jnp.zeros((HALO, WIDE), f32)

    def convolve(h, carry):
        lanes = pl.ds(pl.multiple_of(h * F, F), F)
        ahead = jnp.broadcast_to(taps[pl.ds(core * HEADS + h, 1), :], (HALF, 2 * HALF))
        back = jnp.broadcast_to(taps[pl.ds((2 + core) * HEADS + h, 1), :], (HALF, 2 * HALF))
        ahead = split(pltpu.roll(ahead, 0, 1, stride=1, stride_axis=0)[:, : HALF + 2 * HALO])
        back = split(pltpu.roll(back, 0, 1, stride=1, stride_axis=0)[:, : HALF + 2 * HALO])
        total = jnp.zeros((HALF, 2 * HALF), f32)
        for b in range(2):
            window = pl.ds(b * HALF, HALF + 2 * HALO)
            vw = split(Vs[pl.ds(b * HALF, 2 * HALF), lanes])
            near_v = (vw[0][: HALF + 2 * HALO], vw[1][: HALF + 2 * HALO])
            mixed_s[pl.ds(b * HALF, HALF), lanes] = mm3(ahead, near_v, 1, 0)
            dv_s[pl.ds(b * HALF, HALF), lanes] = mm3(back, split(Gs[window, lanes]), 1, 0)
            total = total + mm3(split(Gs[pl.ds(HALO + b * HALF, HALF), lanes]), vw, 1, 1)
        acc = total[:8]
        for block in range(1, HALF // 8):
            acc = acc + pltpu.roll(total[block * 8:(block + 1) * 8], 2 * HALF - 8 * block, 1)
        line = acc[:1]
        for r in range(1, 8):
            line = line + pltpu.roll(acc[r:r + 1], 2 * HALF - r, 1)
        kgp[h] = jnp.broadcast_to(line[:, :F], (8, F))
        return carry

    def convolutions(first, end):
        lax.fori_loop(first, end, convolve, 0)

    low_rows = lax.broadcasted_iota(jnp.int32, (CHIPS // 2, 8, F), 1) < 4

    def landmarks(j, hh):
        t = marks[j, :, pl.ds(hh, 1)].reshape(2 * M, F)
        r = pltpu.roll(t, 2 * M - 4, 0).reshape(CHIPS // 2, 2, 8, F)
        t = t.reshape(CHIPS // 2, 2, 8, F)
        qm = jnp.where(low_rows, t[:, 0], r[:, 0]).reshape(M, F)
        km = jnp.where(low_rows, r[:, 0], t[:, 1]).reshape(M, F)
        return qm, km

    def combine(pieces):
        tops = [p[2 * QUARTER:2 * QUARTER + 1] for p in pieces]
        top = tops[0]
        for t in tops[1:]:
            top = jnp.maximum(top, t)
        sums, rest, totals = 0.0, 0.0, 0.0
        for p, t in zip(pieces, tops):
            factor = jnp.exp(t - top)
            sums = sums + p[:QUARTER] * factor
            rest = rest + p[QUARTER:2 * QUARTER]
            totals = totals + p[2 * QUARTER + 1:2 * QUARTER + 2] * factor
        return sums, rest, top, totals

    def stats(*rows):
        return jnp.concatenate(list(rows) + [jnp.zeros((8 - len(rows), M), f32)], axis=0)

    def put(ref, index, sums, rest, tile):
        ref[(*index, pl.ds(0, QUARTER))] = sums
        ref[(*index, pl.ds(QUARTER, QUARTER))] = rest
        ref[(*index, pl.ds(2 * QUARTER, 8))] = tile

    def forward_head(j, hh):
        h = 2 * hh + j
        lanes = pl.ds(pl.multiple_of(h * F, F), F)
        qm, km = landmarks(j, hh)
        qm_s[h] = qm
        km_s[h] = km
        scores = mm3(split(Qs[:, lanes]), split(km), 1, 1) * SCALE
        e = jnp.exp(scores - jnp.max(scores, axis=-1, keepdims=True))
        near = e / jnp.sum(e, axis=-1, keepdims=True)
        N_s[h] = near
        scores = mm3(split(Ks[:, lanes]), split(qm), 1, 1) * SCALE
        top = jnp.max(scores, axis=0, keepdims=True)
        e = jnp.exp(scores - top)
        E_s[h] = e
        own = pl.ds(HALO, ROWS)
        summary = mm3(split(Vs[own, lanes]), split(e), 0, 0)
        grad = mm3(split(Gs[own, lanes]), split(near), 0, 0)
        tile = stats(top, jnp.sum(e, axis=0, keepdims=True))
        st_s[h] = tile
        for p in range(4):
            put(parts, (h, p), summary[p * QUARTER:(p + 1) * QUARTER], grad[p * QUARTER:(p + 1) * QUARTER], tile)

    def rs2(j):
        return [
            remote(
                parts.at[2 * ((y + n) % NY) + j], from_rows.at[j, n - 1], rs2s.at[j, n - 1], rs2r.at[j, n - 1],
                dev((y + n) % NY, z),
            )
            for n in range(1, NY)
        ]

    send2 = [rs2(0), rs2(1)]

    def to_z2(j, p):
        return remote(red.at[j, p], zbuf.at[z], rs2zs.at[2 * p + j], rs2zr.at[z], dev(y, 2 * p + j))

    def from_z2(zz):
        return remote(zbuf.at[zz], zbuf.at[zz], rs2zs.at[zz], rs2zr.at[zz], dev(y, zz))

    def settle2(j):
        for c in send2[j]:
            c.wait_recv()

        def one(p, carry):
            sums, rest, top, totals = combine([parts[2 * y + j, p]] + [from_rows[j, n, p] for n in range(NY - 1)])
            put(red, (j, p), sums, rest, stats(top, totals))

            @pl.when(2 * p + j != z)
            def _():
                to_z2(j, p).start()

            @pl.when(2 * p + j == z)
            def _():
                zbuf[z] = red[j, p]

            return carry

        lax.fori_loop(0, 4, one, 0)

    def forward_events():
        return {
            0: [("far", send2[0][1].start)],
            1: [("up", send2[0][0].start)],
            2: [("down", send2[0][2].start)],
            3: [("finish", finish1[1])],
            4: [("far", send2[1][1].start)],
            5: [("up", send2[1][0].start)],
            6: [("down", send2[1][2].start), ("settle", lambda: settle2(0))],
        }

    def run(events, i):
        for at, work in events.items():
            def do(at=at, work=work):
                for name, act in work:
                    act()

            pl.when(i == at)(do)

    def forward_step(i, carry):
        n = i % 4
        turn = jnp.where(n == 0, 2, jnp.where(n == 1, 1, jnp.where(n == 2, 3, 0)))
        forward_head(i // 4, (y + turn) % NY)
        run(forward_events(), i)
        return carry

    lax.fori_loop(0, HEADS, forward_step, 0)

    served = 2 * y + parity
    qm, km = qm_s[served], km_s[served]
    scores = mmf(qm, km, 1, 1) * SCALE
    e = jnp.exp(scores - jnp.max(scores, axis=-1, keepdims=True))
    A = e / jnp.sum(e, axis=-1, keepdims=True)
    eye = (
        lax.broadcasted_iota(jnp.int32, (M, M), 0) == lax.broadcasted_iota(jnp.int32, (M, M), 1)
    ).astype(f32)
    row_sum = jnp.sum(A, axis=1, keepdims=True)
    col_sum = jnp.sum(A, axis=0, keepdims=True)
    row_most = jnp.max(row_sum, axis=0, keepdims=True)
    col_most = jnp.max(col_sum, axis=1, keepdims=True)
    shrink = 1.0 / (row_most * col_most)
    Z = A.T * shrink
    trail = []

    def newton(Z):
        Pm = mmf(A, Z, 1, 0)
        H = 7.0 * eye - Pm
        E = 15.0 * eye - mmf(Pm, H, 1, 0)
        C = 13.0 * eye - mmf(Pm, E, 1, 0)
        trail.append((Z, Pm, H, E, C))
        return 0.25 * mmf(Z, C, 1, 0)

    Z = newton(Z)
    Z = newton(Z)
    Z = newton(Z)

    def serve(j):
        @pl.when(parity == j)
        def _():
            for d in range(1, NZ):
                from_z2((z + d) % NZ).wait_recv()
            sums, weight_grad, top, totals = combine([zbuf[i] for i in range(NZ)])
            summary = sums / totals
            weighted = mmf(summary, Z, 1, 1)
            summary_grad = mmf(weight_grad, Z, 1, 0)
            fdot = jnp.sum(summary_grad * summary, axis=0, keepdims=True)
            put(W3, (chip,), weighted, summary_grad, stats(top, totals, fdot))
            start3[j]()
            served_s[0] = summary
            served_s[1] = weight_grad

    def pull_back():
        summary, weight_grad = served_s[0], served_s[1]
        dZ = mmf(weight_grad, summary, 0, 0)
        dA = jnp.zeros((M, M), f32)
        for turn, (Zi, Pm, H, E, C) in enumerate(reversed(trail)):
            dC = 0.25 * mmf(Zi, dZ, 0, 0)
            dZ = 0.25 * mmf(dZ, C, 1, 1)
            dP = -mmf(dC, E, 1, 1)
            dE = -mmf(Pm, dC, 0, 0)
            dP = dP - mmf(dE, H, 1, 1)
            dH = -mmf(Pm, dE, 0, 0)
            dP = dP - dH
            dA = dA + mmf(dP, Zi, 1, 1)
            dZ = dZ + mmf(A, dP, 0, 0)
        dA = dA + (dZ * shrink).T
        shrink_grad = jnp.sum(jnp.sum(dZ * A.T, axis=1, keepdims=True), axis=0, keepdims=True)
        product_grad = -shrink_grad * shrink * shrink
        row_hit = (row_sum == row_most).astype(f32)
        col_hit = (col_sum == col_most).astype(f32)
        dA = dA + product_grad * col_most * row_hit / jnp.sum(row_hit, axis=0, keepdims=True)
        dA = dA + product_grad * row_most * col_hit / jnp.sum(col_hit, axis=1, keepdims=True)
        middle = A * (dA - jnp.sum(dA * A, axis=-1, keepdims=True)) * SCALE
        fix[0] = mmf(middle, km, 1, 0)
        fix[1] = mmf(middle, qm, 0, 0)

    settle2(1)
    meet_halos()
    convolutions(0, 4)
    serve(0)
    convolutions(4, 6)
    serve(1)
    pull_back()
    for i in range(4):
        step3[0](i)
    convolutions(6, 8)

    def kg_to_z(zz):
        return remote(kgz.at[z], kgz.at[z], kzs.at[zz], kzr.at[z], dev(y, zz))

    def kg_from_z(zz):
        return remote(kgz.at[zz], kgz.at[zz], kzs.at[zz], kzr.at[zz], dev(y, zz))

    def kg_to_y(yy):
        return remote(kgy.at[y], kgy.at[y], kys.at[yy], kyr.at[y], dev(yy, z))

    def kg_from_y(yy):
        return remote(kgy.at[yy], kgy.at[yy], kys.at[yy], kyr.at[yy], dev(yy, z))

    kgz[z] = jnp.concatenate([kgp[h][:1] for h in range(HEADS)], axis=0)
    for d in range(1, NZ):
        kg_to_z((z + d) % NZ).start()

    def kg_second():
        for d in range(1, NZ):
            kg_from_z((z + d) % NZ).wait_recv()
        total = kgz[0]
        for i in range(1, NZ):
            total = total + kgz[i]
        kgy[y] = total
        for d in range(1, NY):
            kg_to_y((y + d) % NY).start()

    taps_out = []
    for dx in range(4):
        for dc in range(2):
            if dx + dc:
                xx, cc = (x + dx) % 4, (core + dc) % 2
                i = dx * 2 + dc
                taps_out.append((
                    remote(kgb.at[core, x], kgb.at[core, x], kgs.at[i], kgr.at[core, x], chip * 2 + cc, xx),
                    remote(kgb.at[cc, xx], kgb.at[cc, xx], kgs.at[i], kgr.at[cc, xx], chip * 2 + cc, xx),
                ))

    def kg_third():
        for d in range(1, NY):
            kg_from_y((y + d) % NY).wait_recv()
        kgb[core, x] = kgy[0] + kgy[1] + kgy[2] + kgy[3]
        for c, _ in taps_out:
            c.start()


    for i in range(4):
        step3[1](i)
    finish3[0]()

    def scattered(a, b):
        first = jnp.where(low_rows, a.reshape(CHIPS // 2, 8, F), pltpu.roll(b, 4, 0).reshape(CHIPS // 2, 8, F))
        second = jnp.where(low_rows, pltpu.roll(a, M - 4, 0).reshape(CHIPS // 2, 8, F), b.reshape(CHIPS // 2, 8, F))
        return jnp.stack([first, second], axis=1).reshape(CHIPS, 8, F)

    def backward_head(j, hh):
        h = 2 * hh + j
        lanes = pl.ds(pl.multiple_of(h * F, F), F)
        own = pl.ds(HALO, ROWS)
        got = [W3[hh * NZ + j + 2 * p] for p in range(4)]
        wt = split(jnp.concatenate([p[:QUARTER] for p in got], axis=0))
        st = split(jnp.concatenate([p[QUARTER:2 * QUARTER] for p in got], axis=0))
        top = got[0][2 * QUARTER:2 * QUARTER + 1]
        totals = got[0][2 * QUARTER + 1:2 * QUARTER + 2]
        fdot = sum(p[2 * QUARTER + 2:2 * QUARTER + 3] for p in got)
        near = N_s[h]
        gs = split(Gs[own, lanes])
        mixed_s[:, lanes] = mixed_s[:, lanes] + mm3(split(near), wt, 1, 1)
        dn = mm3(gs, wt, 1, 0)
        ns = split(near * (dn - jnp.sum(dn * near, axis=-1, keepdims=True)) * SCALE)
        dq_s[:, lanes] = mm3(ns, split(km_s[h]), 1, 0)
        dkm = mm3(ns, split(Qs[:, lanes]), 0, 0)
        far = E_s[h] * (jnp.exp(st_s[h][0:1] - top) / totals)
        dv_s[:, lanes] = dv_s[:, lanes] + mm3(split(far), st, 1, 1)
        df = mm3(split(Vs[own, lanes]), st, 1, 0)
        fs = split(far * (df - fdot) * SCALE)
        dk_s[:, lanes] = mm3(fs, split(qm_s[h]), 1, 0)
        dqm = mm3(fs, split(Ks[:, lanes]), 0, 0)
        share = (h == served).astype(f32)
        out4[h] = scattered(dqm + share * fix[0], dkm + share * fix[1])

    def rs4(i):
        h = 2 * (i % 4) + i // 4
        return [
            remote(
                out4.at[h, pl.ds(((y + n) % NY) * NZ, NZ)], buf4.at[h, n - 1], rs4s.at[n - 1, h], rs4r.at[n - 1, h],
                dev((y + n) % NY, z),
            )
            for n in (2, 1, 3)
        ]

    def to_z4(n, zz):
        return remote(red4.at[n, zz], zbuf4.at[n, z], rs4zs.at[n, zz], rs4zr.at[n, z], dev(y, zz))

    def from_z4(n, zz):
        return remote(red4.at[n, zz], zbuf4.at[n, zz], rs4zs.at[n, zz], rs4zr.at[n, zz], dev(y, zz))

    def settle4(n):
        for e in range(2):
            i = 2 * n + e
            h = 2 * (i % 4) + i // 4
            for c in rs4(i):
                c.wait_recv()
            here = out4[h, pl.ds(y * NZ, NZ)] + buf4[h, 0] + buf4[h, 1] + buf4[h, 2]
            for zz in range(NZ):
                red4[n, zz, e] = here[zz]
        for i in range(1, NZ):
            to_z4(n, (z + NZ + offset(i)) % NZ).start()
        zbuf4[n, z] = red4[n, z]

    def backward_events():
        def send(i):
            for c in rs4(i):
                c.start()

        events = {i: [("send", lambda i=i: send(i))] for i in range(HEADS)}
        events[1] += [("taps", kg_second)]
        events[3] += [("finish", finish3[1])]
        events[5] += [("settle", lambda: settle4(0)), ("taps", kg_third)]
        events[7] += [("settle", lambda: settle4(1))]
        return events

    def backward_step(i, carry):
        backward_head(i // 4, i % 4)
        run(backward_events(), i)
        return carry

    lax.fori_loop(0, HEADS, backward_step, 0)

    outs = []
    for i, (s, t) in enumerate(((mixed_s, mixed_o), (dv_s, dv_o), (dq_s, dq_o), (dk_s, dk_o))):
        outs.append((
            pltpu.make_async_copy(s.at[rows_of(0, core)], t.at[:, mine], os_l.at[i]),
            remote(s.at[rows_of(0, 1 - core)], t.at[:, mine], os_s.at[i], os_r.at[i], sib),
            remote(s.at[rows_of(0, 1 - core)], t.at[:, theirs], os_s.at[i], os_r.at[i], sib),
        ))
    for a, b, _ in outs:
        a.start()
        b.start()
    settle4(2)
    settle4(3)
    for _, c in taps_out:
        c.wait_recv()
    kg_o[...] = jnp.concatenate([kgb[c, 0] + kgb[c, 1] + kgb[c, 2] + kgb[c, 3] for c in range(2)], axis=0)
    for n in range(HEADS // 2):
        for i in range(1, NZ):
            from_z4(n, (z + NZ + offset(i)) % NZ).wait_recv()
        for e in range(2):
            i = 2 * n + e
            h = 2 * (i % 4) + i // 4
            total = zbuf4[n, 0, e]
            for zz in range(1, NZ):
                total = total + zbuf4[n, zz, e]
            fin[:, h * F:(h + 1) * F] = total * (1.0 / SEGMENT)
    marks_out = (
        pltpu.make_async_copy(fin, marks_o.at[:, mine], os_l.at[4]),
        remote(fin, marks_o.at[:, mine], os_s.at[4], os_r.at[4], sib),
        remote(fin, marks_o.at[:, theirs], os_s.at[4], os_r.at[4], sib),
    )
    marks_out[0].start()
    marks_out[1].start()
    outs.append(marks_out)

    mark_in.wait_send()
    for c in sib_in:
        c.wait_send()
    for c in halos:
        c.wait_send()
    for j in range(2):
        drain1[j]()
        drain3[j]()
        for c in send2[j]:
            c.wait_send()
        for p in range(4):
            pl.when(2 * p + j != z)(lambda j=j, p=p: to_z2(j, p).wait_send())
    for d in range(1, NZ):
        kg_to_z((z + d) % NZ).wait_send()
    for d in range(1, NY):
        kg_to_y((y + d) % NY).wait_send()

    for n in range(HEADS // 2):
        for d in range(1, NZ):
            to_z4(n, (z + d) % NZ).wait_send()
    for i in range(HEADS):
        for c in rs4(i):
            c.wait_send()
    for c, _ in taps_out:
        c.wait_send()
    for a, b, c in outs:
        a.wait()
        b.wait_send()
        c.wait_recv()


def finish(scale, mixed, dq, dk, dv, marks, kg, mixed_o, dq_o, dk_o, dv_o, kg_o, dq_s, dk_s, sem):
    core = lax.axis_index("ctx") % 2
    copies = [pltpu.make_async_copy(mixed, mixed_o, sem.at[0]), pltpu.make_async_copy(dv, dv_o, sem.at[1])]
    for c in copies:
        c.start()
    for n, (part, whole, out) in enumerate(((dq, dq_s, dq_o), (dk, dk_s, dk_o))):
        for m in range(2):
            picked = marks[pl.ds(4 * n + m, 1), :]
            other = marks[pl.ds(4 * n + 2 + m, 1), :]
            row = jnp.where(core == 0, picked, other)
            positions = pl.ds(m * SEGMENT, SEGMENT)
            whole[positions, :] = part[positions, :] + row
        copies.append(pltpu.make_async_copy(whole, out, sem.at[2 + n]))
        copies[-1].start()
    kg_o[...] = kg[:, :TAPS] * scale
    for c in copies:
        c.wait()


def layer(queries, keys, values, kernel_taps, cotangent):
    rows, wide = queries.shape[1:]
    DMA = pltpu.SemaphoreType.DMA

    def vm(*shape):
        return pltpu.VMEM(shape, f32)

    anywhere = pl.BlockSpec(memory_space=pl.ANY)
    vmem = pl.BlockSpec(memory_space=pltpu.VMEM)
    big = jax.ShapeDtypeStruct((rows, wide), f32)
    outs = pl.pallas_call(
        kernel,
        out_shape=(big, big, big, big, jax.ShapeDtypeStruct((8, wide), f32), jax.ShapeDtypeStruct((2 * HEADS, F), f32)),
        in_specs=[pl.BlockSpec(memory_space=pltpu.HBM)] * 5,
        out_specs=(anywhere,) * 5 + (vmem,),
        scratch_shapes=[
            vm(HALF, 2 * WIDE), vm(HALF, 2 * WIDE), vm(2, 2, HALF_HEADS, 8, F), vm(2, HALF_HEADS, 8, F),
            vm(2 * HEADS, TAPS), vm(4 * HEADS, 2 * HALF),
            vm(ROWS, WIDE), vm(ROWS, WIDE), vm(3 * HALF, WIDE), vm(ROWS + 2 * HALO, WIDE),
            vm(2, CHIPS, HALF_HEADS, 8, F), vm(HEADS, M, F), vm(HEADS, M, F), vm(HEADS, ROWS, M), vm(HEADS, ROWS, M),
            vm(HEADS, 8, M), vm(HEADS, 8, F), vm(ROWS, WIDE), vm(ROWS, WIDE), vm(ROWS, WIDE), vm(ROWS, WIDE),
            vm(HEADS, 4, PIECE, M), vm(2, NY - 1, 4, PIECE, M),
            vm(2, 4, PIECE, M), vm(NZ, PIECE, M), vm(CHIPS, PIECE, M), vm(2, QUARTER, M), vm(2, M, F),
            vm(HEADS, CHIPS, 8, F), vm(HEADS, NY - 1, NZ, 8, F),
            vm(HEADS // 2, NZ, 2, 8, F), vm(HEADS // 2, NZ, 2, 8, F), vm(8, WIDE),
            vm(NZ, HEADS, F), vm(NY, HEADS, F), vm(2, 4, HEADS, F),
            DMA((7,)), DMA((5,)), DMA((5,)), DMA((4,)), DMA((4,)), DMA((2, 2, NY, NZ)), DMA((2, 2, NY, NZ)),
            DMA((2, NY - 1)), DMA((2, NY - 1)), DMA((NZ,)), DMA((NZ,)), DMA((3, HEADS)), DMA((3, HEADS)),
            DMA((HEADS // 2, NZ)), DMA((HEADS // 2, NZ)), DMA((5,)), DMA((5,)), DMA((5,)),
            DMA((NZ,)), DMA((NZ,)), DMA((NY,)), DMA((NY,)), DMA((8,)), DMA((2, 4)),
        ],
        compiler_params=pltpu.CompilerParams(
            collective_id=0, has_side_effects=True, vmem_limit_bytes=48 * 1024 * 1024
        ),
    )(*[pltpu.with_memory_space_constraint(a, pltpu.HBM) for a in (queries[0], keys[0], values[0], cotangent[0], kernel_taps)])
    total = lax.axis_size("batch") * lax.axis_size("ctx") * rows * F
    mixed, dq, dk, dv, kg = pl.pallas_call(
        functools.partial(finish, 1.0 / math.sqrt(total)),
        out_shape=(big, big, big, big, jax.ShapeDtypeStruct((2 * HEADS, TAPS), f32)),
        in_specs=[vmem] * 6,
        out_specs=(anywhere,) * 4 + (vmem,),
        scratch_shapes=[vm(rows, wide), vm(rows, wide), DMA((4,))],
        compiler_params=pltpu.CompilerParams(vmem_limit_bytes=12 * 1024 * 1024),
    )(*outs)
    return mixed[None], dq[None], dk[None], dv[None], kg


def solution(mesh):
    block = P("batch", "ctx", None)
    return jax.shard_map(
        layer, mesh=mesh, in_specs=(block, block, block, P(), block),
        out_specs=(block, block, block, block, P()), check_vma=False,
    )
```
